32 devices in a mesh: groups: 2 (over y), mp: 4 (over z), layer: 2 (over x), pool: 2 (over core).
Axes of the slice: x: 2, y: 2, z: 4, core: 2. Of those that a mesh axis runs over, the one named last changes fastest.
Arguments:
- enc_rows: float32 [2048, 4096], P(('groups', 'mp', 'layer', 'pool')), parts along dimension 0, may hold values from -6 to 6
- kv_weight: bfloat16 [2, 4096, 2, 4096], P('layer', 'pool', None, 'mp'), may hold values from -0.09375 to 0.09375
- lengths: int32 [32], P('groups'), parts along dimension 0, may hold values from 1 to 128, 1024 in all
- slot_of: int32 [32], P('groups'), parts along dimension 0, may hold values from 0 to 15, each once
- order: int32 [32], P('groups'), parts along dimension 0, may hold values from 0 to 15, each once
Outputs:
- kv_cache: bfloat16 [2, 32, 128, 2, 4096], P('layer', ('groups', 'pool'), None, None, 'mp'), parts along dimension 1
The draws below stay inside these ranges and needn't reach their ends.
There are 2 independent parts, one for each index of `groups`. The reference program is written for one: setup_inputs(seed, part) draws one part's arguments, and reference() takes and returns one part's arrays. A program takes and returns all parts, laid end to end along the dimension named above; an argument that names none is the same for every part. Nothing has to cross between parts.
Inputs may be any that keep to these rules, and one draw needn't show every extreme that they name: The 16 lengths add up to exactly 1024, and some request has exactly 128 rows. `slot_of`: a permutation of the 16 slots. A permutation of the 16 requests; their rows lie in enc_rows one request after another in this order.
All inputs are finite; a program needn't handle non-finite values.
Results may differ from the reference program's by a relative error of at most 0.0049.
Values may be sent and summed in bfloat16 or wider, within the bound.
A program may use at most 128 MiB of HBM per device.

```python
import math
import jax
import jax.numpy as jnp
import numpy as np
from jax import lax

D = 4096
SLOTS = 16
MAXLEN = 128
PACK = 1024
LAYERS = 2


def level_of(own_key, extent, split, low, largest):
    def one(dim, blocks):
        steps = jax.random.uniform(jax.random.fold_in(jax.random.fold_in(own_key, 6), dim), (blocks,), jnp.float32, low / len(split), largest / len(split))
        return jnp.repeat(jnp.exp(steps), extent[dim] // blocks).reshape((-1,) + (1,) * (len(extent) - dim - 1))

    gain = one(*split[0])
    for cut in split[1:]:
        gain = gain * one(*cut)
    return gain


def split_up(amount, total, reach, lean):
    loads = [(1 << 20) // math.isqrt(grade ** lean) + 1 for grade in range(2, amount + 1)]
    rest, counts = total - reach - (amount - 1), [1] * (amount - 1)
    while rest > 0:
        candidates = [i for i in range(amount - 1) if counts[i] < reach]
        whole, remaining = sum([loads[i] for i in candidates]), rest
        for i in candidates:
            more = min(reach - counts[i], max(1, remaining * loads[i] // whole), rest)
            counts[i] = counts[i] + more
            rest = rest - more
    return np.array([reach] + counts)


def uneven(stream_key, number_of, total, reach, skew):
    if number_of == 2:
        one = jax.random.randint(stream_key, (), max(1, total - reach), min(reach, total - 1) + 1)
        return jnp.stack([one, total - one])
    sizes = jnp.asarray(split_up(number_of, total, reach, skew), jnp.int32)
    pairs = (number_of - 1) // 2
    donor, sink = sizes[1:1 + 2 * pairs:2], sizes[2:2 + 2 * pairs:2]
    margin = jnp.minimum(donor - 1, reach - sink)
    moved = jax.random.randint(jax.random.fold_in(stream_key, 1), (pairs,), 0, 1 << 20) % (margin + 1)
    sizes = sizes.at[1:1 + 2 * pairs:2].set(donor - moved).at[2:2 + 2 * pairs:2].set(sink + moved)
    return sizes[jax.random.permutation(jax.random.fold_in(stream_key, 2), number_of)]


def noise(stream_key, extent, width, most, cuts=(), kind=jnp.bfloat16):
    result = jax.random.normal(stream_key, extent, jnp.float32) * width
    if len(cuts) > 0:
        result = level_of(stream_key, extent, cuts, -0.22, 0.18) * result
    return jnp.clip(result, min=-most, max=most).astype(kind)


def setup_inputs(seed: int = 0, part: int = 0) -> dict:
    seeds = jax.random.split(jax.random.key(seed), 6)
    part_keys = jax.random.split(jax.random.fold_in(seeds[5], part), 6)
    return {
        "enc_rows": noise(part_keys[0], (PACK, D), 1.0, 6.0, ((0, 16),), jnp.float32),
        "kv_weight": noise(seeds[1], (LAYERS, D, 2, D), D ** -0.5, 0.09375, ((0, 2), (1, 2), (3, 4))),
        "lengths": uneven(part_keys[2], SLOTS, PACK, MAXLEN, 2).astype(jnp.int32),
        "slot_of": jax.random.permutation(part_keys[3], SLOTS).astype(jnp.int32),
        "order": jax.random.permutation(part_keys[4], SLOTS).astype(jnp.int32),
    }


def reference(enc_rows, kv_weight, lengths, slot_of, order):
    row_block = enc_rows.astype(jnp.bfloat16)
    order_length = lengths[order]
    order_begin = jnp.cumsum(order_length) - order_length
    begins = jnp.zeros((SLOTS,), jnp.int32).at[order].set(order_begin.astype(jnp.int32))
    request = jnp.zeros((SLOTS,), jnp.int32).at[slot_of].set(jnp.arange(SLOTS, dtype=jnp.int32))
    position = jnp.arange(MAXLEN, dtype=jnp.int32)
    inside = position[None, :] < lengths[request][:, None]
    source = jnp.where(inside, begins[request][:, None] + position[None, :], 0).astype(jnp.int32)

    def one_layer(layer_weight):
        flat_weight = layer_weight.reshape(D, 2 * D)
        key_value = jnp.dot(row_block, flat_weight, preferred_element_type=jnp.float32).astype(jnp.bfloat16)
        placed = jnp.take(key_value, source.reshape(-1), axis=0).reshape(SLOTS, MAXLEN, 2, D)
        return jnp.where(inside[:, :, None, None], placed, jnp.zeros((), jnp.bfloat16))

    return lax.map(one_layer, kv_weight)
```

```python
import functools

import jax
import jax.numpy as jnp
from jax import lax
from jax.experimental import pallas as pl
from jax.experimental.pallas import tpu as pltpu
from jax.sharding import PartitionSpec as P
MAXLEN = 128


def pack_tables(lengths, slot_of, order):
    count_all = lengths.shape[0]
    request_ids = lax.iota(jnp.int32, count_all)
    selector = (order[:, None] == request_ids[None, :]).astype(jnp.int32)
    order_length = jnp.sum(selector * lengths[None, :], axis=1)
    order_begin = jnp.cumsum(order_length) - order_length
    begins = jnp.sum(selector * order_begin[:, None], axis=0)
    owner = (slot_of[:, None] == request_ids[None, :]).astype(jnp.int32)
    request = jnp.sum(owner * request_ids[:, None], axis=0)
    chooser = (request[:, None] == request_ids[None, :]).astype(jnp.int32)
    slot_begin = jnp.sum(chooser * begins[None, :], axis=1)
    slot_size = jnp.sum(chooser * lengths[None, :], axis=1)
    return (slot_begin, slot_size)


def place_rows(values, positions, slot_begin, slot_size):
    slot_count = slot_begin.shape[0]
    slot_index = positions // MAXLEN
    offset = positions % MAXLEN
    selector = (slot_index[:, None] == lax.iota(jnp.int32, slot_count)[None, :]).astype(jnp.int32)
    first_row = jnp.sum(selector * slot_begin[None, :], axis=1)
    row_limit = jnp.sum(selector * slot_size[None, :], axis=1)
    inside = offset < row_limit
    source = jnp.where(inside, first_row + offset, 0)
    taken = jnp.take(values, source, axis=0)
    return jnp.where(inside[:, None], taken, jnp.zeros((), values.dtype))


def gather_multiply(mp_size, x_ref, w_hbm, kv_ref, w_raw, w_flat, x_send, rows, acc, part, other, *sems):
    w_sem, x_ss, x_rs, r_ss, r_rs, l_ss, l_rs, p_ss, p_rs = sems
    mesh_id = pl.DeviceIdType.MESH
    ring = 2 * mp_size
    count, half = x_send.shape
    width = w_flat.shape[1]
    pool = lax.axis_index("pool")
    layer = lax.axis_index("layer")
    mp = lax.axis_index("mp")
    here = mp + layer * (ring - 1 - 2 * mp)

    def place(steps):
        at = (here + steps + ring) % ring
        on_layer = at // mp_size
        return at + on_layer * (ring - 1 - 2 * at), on_layer

    def chip(steps):
        on_mp, on_layer = place(steps)
        return on_mp * 2 + on_layer

    def device(steps):
        on_mp, on_layer = place(steps)
        return {"mp": on_mp, "layer": on_layer}

    partner = {"pool": 1 - pool}
    depth = half // 4

    def weight_copy(i):
        return pltpu.make_async_copy(
            w_hbm.at[pl.ds(i * depth, depth)], w_raw.at[pl.ds(i * depth, depth)], w_sem.at[i]
        )

    for i in range(4):
        weight_copy(i).start()
    barrier = pltpu.get_barrier_semaphore()
    for target in (device(1), device(-1), partner):
        pl.semaphore_signal(barrier, inc=1, device_id=target, device_id_type=mesh_id)
    mine = chip(0)
    rows[mine, pool] = x_ref[:, pl.ds(pl.multiple_of(pool * half, half), half)].astype(jnp.bfloat16)
    x_send[...] = x_ref[:, pl.ds(pl.multiple_of((1 - pool) * half, half), half)].astype(jnp.bfloat16)
    pl.semaphore_wait(barrier, 3)

    def send(k, direction):
        last = k == ring - 2
        second = (k % 2 == 1) or (last and direction < 0)
        core = 1 - pool if second else pool
        slot = rows.at[chip(-direction * (k // 2)), core]
        ss, rs = (r_ss, r_rs) if direction > 0 else (l_ss, l_rs)
        return pltpu.make_async_remote_copy(
            src_ref=slot, dst_ref=slot, send_sem=ss.at[k], recv_sem=rs.at[k],
            device_id=device(direction), device_id_type=mesh_id,
        )

    def swap_rows():
        return pltpu.make_async_remote_copy(
            src_ref=x_send, dst_ref=rows.at[mine, pool], send_sem=x_ss, recv_sem=x_rs,
            device_id=partner, device_id_type=mesh_id,
        )

    def arrived(k, direction):
        last = k == ring - 2
        second = (k % 2 == 1) or (last and direction < 0)
        core = 1 - pool if second else pool
        slot = rows.at[chip(-direction * (k // 2 + 1)), core]
        ss, rs = (r_ss, r_rs) if direction > 0 else (l_ss, l_rs)
        pltpu.make_async_remote_copy(
            src_ref=slot, dst_ref=slot, send_sem=ss.at[k], recv_sem=rs.at[k],
            device_id=device(direction), device_id_type=mesh_id,
        ).wait_recv()

    def flatten(i):
        weight_copy(i).wait()
        piece = 32

        @pl.loop(0, depth // piece)
        def _(t):
            start = pl.multiple_of(i * depth + t * piece, piece)
            w_flat[pl.ds(start, piece), :] = w_raw[pl.ds(start, piece)].reshape(piece, width)

    def swap_part(m, at):
        return pltpu.make_async_remote_copy(
            src_ref=part.at[at], dst_ref=other.at[at], send_sem=p_ss.at[m], recv_sem=p_rs.at[m],
            device_id=partner, device_id_type=mesh_id,
        )

    def multiply(chips, m):
        columns = 256

        @pl.loop(0, width // columns)
        def _(t):
            span = pl.ds(pl.multiple_of(t * columns, columns), columns)
            left = jnp.concatenate([rows[c].reshape(2 * count, half) for c in chips], axis=0)
            product = jnp.dot(left, w_flat[:, span], preferred_element_type=jnp.float32)
            for i, c in enumerate(chips):
                one = product[i * 2 * count : (i + 1) * 2 * count]
                acc[c, :, span] = one
                part[c, :, span] = one.astype(jnp.bfloat16)

        for i, c in enumerate(chips):
            swap_part(m + i, c).start()

    def finish(chips, m):
        for i, c in enumerate(chips):
            swap_part(m + i, c).wait_recv()

            @pl.loop(0, 2 * count // 16)
            def _(t):
                span = pl.ds(pl.multiple_of(t * 16, 16), 16)
                total = acc[c, span, :] + other[c, span, :].astype(jnp.float32)
                kv_ref[c, span, :] = total.astype(jnp.bfloat16)

    send(0, 1).start()
    send(0, -1).start()
    swap_rows().start()
    swap_rows().wait_recv()
    send(1, 1).start()
    send(1, -1).start()
    flatten(0)
    flatten(1)
    reach = ring // 2
    waiting = None
    for k in range(ring - 1):
        if k == ring - 2:
            finish(*waiting)
        arrived(k, 1)
        arrived(k, -1)
        ahead = k + 2
        if ahead < ring - 2:
            send(ahead, 1).start()
            send(ahead, -1).start()
        elif ahead == ring - 2:
            send(ahead, 1).start()
        elif ahead == ring - 1:
            send(ring - 2, -1).start()
        if k == 0:
            flatten(2)
            flatten(3)
            multiply([mine], 0)
            waiting = ([mine], 0)
        elif k % 2 == 1:
            d = (k + 1) // 2
            chips = [chip(-d), chip(d)]
            multiply(chips, 2 * d - 1)
            finish(*waiting)
            waiting = (chips, 2 * d - 1)
    multiply([chip(reach)], ring - 1)
    finish([chip(reach)], ring - 1)
    swap_rows().wait_send()
    for k in range(ring - 1):
        send(k, 1).wait_send()
        send(k, -1).wait_send()
    swap_part(0, mine).wait_send()
    for d in range(1, reach):
        swap_part(2 * d - 1, chip(-d)).wait_send()
        swap_part(2 * d, chip(d)).wait_send()
    swap_part(ring - 1, chip(reach)).wait_send()


def key_values(enc_rows, weight, mp_size):
    count, features = enc_rows.shape
    half, _, head_width = weight.shape
    width, ring = 2 * head_width, 2 * mp_size
    dma = pltpu.SemaphoreType.DMA
    block = (ring, 2 * count, width)
    packed = pl.pallas_call(
        functools.partial(gather_multiply, mp_size),
        out_shape=jax.ShapeDtypeStruct(block, jnp.bfloat16),
        in_specs=[pl.BlockSpec(memory_space=pltpu.VMEM), pl.BlockSpec(memory_space=pl.ANY)],
        out_specs=pl.BlockSpec(memory_space=pltpu.VMEM),
        scratch_shapes=[
            pltpu.VMEM(weight.shape, jnp.bfloat16),
            pltpu.VMEM((half, width), jnp.bfloat16),
            pltpu.VMEM((count, half), jnp.bfloat16),
            pltpu.VMEM((ring, 2, count, half), jnp.bfloat16),
            pltpu.VMEM(block, jnp.float32),
            pltpu.VMEM(block, jnp.bfloat16),
            pltpu.VMEM(block, jnp.bfloat16),
            dma((4,)),
            dma,
            dma,
            dma((ring - 1,)),
            dma((ring - 1,)),
            dma((ring - 1,)),
            dma((ring - 1,)),
            dma((ring,)),
            dma((ring,)),
        ],
        compiler_params=pltpu.CompilerParams(
            collective_id=0, has_side_effects=True, vmem_limit_bytes=56 << 20
        ),
        name="gather_multiply",
    )(enc_rows, weight)
    return packed.reshape(ring * 2 * count, width)


def place_kernel(window, lengths, slot_of, order, kv_ref, out_ref, begins, request):
    slot_count = lengths.shape[0]
    step = pl.program_id(0)

    @pl.when(step == 0)
    def _():
        def one(i, begin):
            begins[order[i]] = begin
            request[slot_of[i]] = i
            return begin + lengths[order[i]]

        lax.fori_loop(0, slot_count, one, jnp.int32(0))

    who = request[lax.axis_index("pool") * pl.num_programs(0) + step]
    size, begin = lengths[who], begins[who]
    base = pl.multiple_of(jnp.minimum((begin // 16) * 16, kv_ref.shape[0] - window), 16)
    shape = (MAXLEN, window)
    position = lax.broadcasted_iota(jnp.int32, shape, 0)
    source = lax.broadcasted_iota(jnp.int32, shape, 1)
    chosen = (source == position + (begin - base)) & (position < size)
    picked = jnp.where(chosen, 1.0, 0.0).astype(jnp.bfloat16)
    taken = jnp.dot(picked, kv_ref[pl.ds(base, window), :], preferred_element_type=jnp.float32)
    out_ref[0, 0] = taken.astype(jnp.bfloat16).reshape(out_ref.shape[2:])


def place_slots(key_value, lengths, slot_of, order, half_slots):
    width = key_value.shape[1]
    slot_count = lengths.shape[0]
    smem = pl.BlockSpec(memory_space=pltpu.SMEM)
    shape = (1, half_slots, MAXLEN, 2, width // 2)
    return pl.pallas_call(
        functools.partial(place_kernel, 2 * MAXLEN),
        grid=(half_slots,),
        out_shape=jax.ShapeDtypeStruct(shape, jnp.bfloat16),
        in_specs=[smem, smem, smem, pl.BlockSpec(memory_space=pltpu.VMEM)],
        out_specs=pl.BlockSpec((1, 1, MAXLEN, 2, width // 2), lambda s: (0, s, 0, 0, 0)),
        scratch_shapes=[
            pltpu.SMEM((slot_count,), jnp.int32),
            pltpu.SMEM((slot_count,), jnp.int32),
        ],
        compiler_params=pltpu.CompilerParams(vmem_limit_bytes=32 << 20),
        name="place_slots",
    )(lengths, slot_of, order, key_value)


def per_device(enc_rows, kv_weight, lengths, slot_of, order):
    half_slots = lengths.shape[0] // lax.axis_size("pool")
    head_width = kv_weight.shape[3]
    mp_size = lax.axis_size("mp")
    ring_fits = (
        lax.axis_size("layer") == 2
        and lax.axis_size("pool") == 2
        and 2 <= mp_size <= 8
        and enc_rows.shape[0] % 16 == 0
        and head_width % 128 == 0
    )
    if ring_fits:
        key_value = key_values(enc_rows, kv_weight[0], mp_size)
        return place_slots(key_value, lengths, slot_of, order, half_slots)
    slot_begin, slot_size = pack_tables(lengths, slot_of, order)
    row_block = enc_rows.astype(jnp.bfloat16)
    weight = lax.all_gather(kv_weight[0], "pool", axis=0, tiled=True)
    flat_weight = weight.reshape(weight.shape[0], 2 * head_width)
    key_value = jnp.dot(
        lax.all_gather(row_block, ("mp", "layer", "pool"), axis=0, tiled=True),
        flat_weight,
        preferred_element_type=jnp.float32,
    ).astype(jnp.bfloat16)
    own_slots = lax.axis_index("pool") * (half_slots * MAXLEN) + lax.iota(
        jnp.int32, half_slots * MAXLEN
    )
    placed = place_rows(key_value, own_slots, slot_begin, slot_size)
    return placed.reshape(1, half_slots, MAXLEN, 2, head_width)


def solution(mesh):
    return jax.shard_map(
        per_device,
        mesh=mesh,
        in_specs=(
            P(("groups", "mp", "layer", "pool"), None),
            P("layer", "pool", None, "mp"),
            P("groups"),
            P("groups"),
            P("groups"),
        ),
        out_specs=P("layer", ("groups", "pool"), None, None, "mp"),
        check_vma=False,
    )
```

```python
import functools

import jax
import jax.numpy as jnp
from jax import lax
from jax.experimental import pallas as pl
from jax.experimental.pallas import tpu as pltpu
from jax.sharding import PartitionSpec as P
MAXLEN = 128


def pack_tables(lengths, slot_of, order):
    count_all = lengths.shape[0]
    request_ids = lax.iota(jnp.int32, count_all)
    selector = (order[:, None] == request_ids[None, :]).astype(jnp.int32)
    order_length = jnp.sum(selector * lengths[None, :], axis=1)
    order_begin = jnp.cumsum(order_length) - order_length
    begins = jnp.sum(selector * order_begin[:, None], axis=0)
    owner = (slot_of[:, None] == request_ids[None, :]).astype(jnp.int32)
    request = jnp.sum(owner * request_ids[:, None], axis=0)
    chooser = (request[:, None] == request_ids[None, :]).astype(jnp.int32)
    slot_begin = jnp.sum(chooser * begins[None, :], axis=1)
    slot_size = jnp.sum(chooser * lengths[None, :], axis=1)
    return (slot_begin, slot_size)


def place_rows(values, positions, slot_begin, slot_size):
    slot_count = slot_begin.shape[0]
    slot_index = positions // MAXLEN
    offset = positions % MAXLEN
    selector = (slot_index[:, None] == lax.iota(jnp.int32, slot_count)[None, :]).astype(jnp.int32)
    first_row = jnp.sum(selector * slot_begin[None, :], axis=1)
    row_limit = jnp.sum(selector * slot_size[None, :], axis=1)
    inside = offset < row_limit
    source = jnp.where(inside, first_row + offset, 0)
    taken = jnp.take(values, source, axis=0)
    return jnp.where(inside[:, None], taken, jnp.zeros((), values.dtype))


def gather_multiply(mp_size, x_ref, w_hbm, kv_hbm, w_raw, w_flat, x_send, rows, acc, part, other, done, *sems):
    w_sem, x_ss, x_rs, r_ss, r_rs, l_ss, l_rs, p_ss, p_rs, o_sem = sems
    mesh_id = pl.DeviceIdType.MESH
    ring = 2 * mp_size
    count, half = x_send.shape
    width = w_flat.shape[1]
    pool = lax.axis_index("pool")
    layer = lax.axis_index("layer")
    mp = lax.axis_index("mp")
    here = mp + layer * (ring - 1 - 2 * mp)

    def place(steps):
        at = (here + steps + ring) % ring
        on_layer = at // mp_size
        return at + on_layer * (ring - 1 - 2 * at), on_layer

    def chip(steps):
        on_mp, on_layer = place(steps)
        return on_mp * 2 + on_layer

    def device(steps):
        on_mp, on_layer = place(steps)
        return {"mp": on_mp, "layer": on_layer}

    partner = {"pool": 1 - pool}
    depth = half // 4

    def weight_copy(i):
        return pltpu.make_async_copy(
            w_hbm.at[pl.ds(i * depth, depth)], w_raw.at[pl.ds(i * depth, depth)], w_sem.at[i]
        )

    for i in range(4):
        weight_copy(i).start()
    barrier = pltpu.get_barrier_semaphore()
    for target in (device(1), device(-1), partner):
        pl.semaphore_signal(barrier, inc=1, device_id=target, device_id_type=mesh_id)
    mine = chip(0)
    rows[mine, pool] = x_ref[:, pl.ds(pl.multiple_of(pool * half, half), half)].astype(jnp.bfloat16)
    x_send[...] = x_ref[:, pl.ds(pl.multiple_of((1 - pool) * half, half), half)].astype(jnp.bfloat16)
    pl.semaphore_wait(barrier, 3)

    def send(k, direction):
        last = k == ring - 2
        second = (k % 2 == 1) or (last and direction < 0)
        core = 1 - pool if second else pool
        slot = rows.at[chip(-direction * (k // 2)), core]
        ss, rs = (r_ss, r_rs) if direction > 0 else (l_ss, l_rs)
        return pltpu.make_async_remote_copy(
            src_ref=slot, dst_ref=slot, send_sem=ss.at[k], recv_sem=rs.at[k],
            device_id=device(direction), device_id_type=mesh_id,
        )

    def swap_rows():
        return pltpu.make_async_remote_copy(
            src_ref=x_send, dst_ref=rows.at[mine, pool], send_sem=x_ss, recv_sem=x_rs,
            device_id=partner, device_id_type=mesh_id,
        )

    def arrived(k, direction):
        last = k == ring - 2
        second = (k % 2 == 1) or (last and direction < 0)
        core = 1 - pool if second else pool
        slot = rows.at[chip(-direction * (k // 2 + 1)), core]
        ss, rs = (r_ss, r_rs) if direction > 0 else (l_ss, l_rs)
        pltpu.make_async_remote_copy(
            src_ref=slot, dst_ref=slot, send_sem=ss.at[k], recv_sem=rs.at[k],
            device_id=device(direction), device_id_type=mesh_id,
        ).wait_recv()

    def flatten(i):
        weight_copy(i).wait()
        piece = 32

        @pl.loop(0, depth // piece)
        def _(t):
            start = pl.multiple_of(i * depth + t * piece, piece)
            w_flat[pl.ds(start, piece), :] = w_raw[pl.ds(start, piece)].reshape(piece, width)

    def swap_part(m, at, side):
        return pltpu.make_async_remote_copy(
            src_ref=part.at[at, side], dst_ref=other.at[at, side],
            send_sem=p_ss.at[m, side], recv_sem=p_rs.at[m, side],
            device_id=partner, device_id_type=mesh_id,
        )

    def store(m, at, side):
        rows_at = pl.ds(pl.multiple_of(at * 2 * count, 2 * count), 2 * count)
        return pltpu.make_async_copy(
            done.at[at, side], kv_hbm.at[side, rows_at, :], o_sem.at[m, side]
        )

    side_width = width // 2
    columns = 256 if side_width % 256 == 0 else 128

    def multiply(chips, m):
        for side in range(2):

            @pl.loop(0, side_width // columns)
            def _(t):
                start = pl.multiple_of(t * columns, columns)
                span = pl.ds(start, columns)
                wide = pl.ds(pl.multiple_of(side * side_width + start, columns), columns)
                left = jnp.concatenate([rows[c].reshape(2 * count, half) for c in chips], axis=0)
                product = jnp.dot(left, w_flat[:, wide], preferred_element_type=jnp.float32)
                for i, c in enumerate(chips):
                    one = product[i * 2 * count : (i + 1) * 2 * count]
                    acc[c, side, :, span] = one
                    part[c, side, :, span] = one.astype(jnp.bfloat16)

            for i, c in enumerate(chips):
                swap_part(m + i, c, side).start()

    def finish(chips, m):
        for side in range(2):
            for i, c in enumerate(chips):
                swap_part(m + i, c, side).wait_recv()

                @pl.loop(0, 2 * count // 32)
                def _(t):
                    span = pl.ds(pl.multiple_of(t * 32, 32), 32)
                    total = acc[c, side, span, :] + other[c, side, span, :].astype(jnp.float32)
                    done[c, side, span, :] = total.astype(jnp.bfloat16)

                store(m + i, c, side).start()

    send(0, 1).start()
    send(0, -1).start()
    swap_rows().start()
    swap_rows().wait_recv()
    send(1, 1).start()
    send(1, -1).start()
    flatten(0)
    flatten(1)
    reach = ring // 2
    waiting = None
    for k in range(ring - 1):
        if k == ring - 2:
            finish(*waiting)
        ahead = k + 2
        arrived(k, 1)
        if ahead <= ring - 2:
            send(ahead, 1).start()
        arrived(k, -1)
        if ahead < ring - 2:
            send(ahead, -1).start()
        elif ahead == ring - 1:
            send(ring - 2, -1).start()
        if k == 0:
            flatten(2)
            flatten(3)
            multiply([mine], 0)
            waiting = ([mine], 0)
        elif k % 2 == 1:
            d = (k + 1) // 2
            chips = [chip(-d), chip(d)]
            if d == 1:
                finish(*waiting)
            multiply(chips, 2 * d - 1)
            waiting = (chips, 2 * d - 1)
        elif k < ring - 2:
            finish(*waiting)
    multiply([chip(reach)], ring - 1)
    finish([chip(reach)], ring - 1)
    swap_rows().wait_send()
    for k in range(ring - 1):
        send(k, 1).wait_send()
        send(k, -1).wait_send()
    blocks = [mine]
    for d in range(1, reach):
        blocks += [chip(-d), chip(d)]
    for m, c in enumerate(blocks + [chip(reach)]):
        for side in range(2):
            swap_part(m, c, side).wait_send()
            store(m, c, side).wait()


def key_values(enc_rows, weight, mp_size):
    count, features = enc_rows.shape
    half, _, head_width = weight.shape
    width, ring = 2 * head_width, 2 * mp_size
    dma = pltpu.SemaphoreType.DMA
    block = (ring, 2, 2 * count, head_width)
    return pl.pallas_call(
        functools.partial(gather_multiply, mp_size),
        out_shape=jax.ShapeDtypeStruct((2, ring * 2 * count, head_width), jnp.bfloat16),
        in_specs=[pl.BlockSpec(memory_space=pltpu.VMEM), pl.BlockSpec(memory_space=pl.ANY)],
        out_specs=pl.BlockSpec(memory_space=pl.ANY),
        scratch_shapes=[
            pltpu.VMEM(weight.shape, jnp.bfloat16),
            pltpu.VMEM((half, width), jnp.bfloat16),
            pltpu.VMEM((count, half), jnp.bfloat16),
            pltpu.VMEM((ring, 2, count, half), jnp.bfloat16),
            pltpu.VMEM(block, jnp.float32),
            pltpu.VMEM(block, jnp.bfloat16),
            pltpu.VMEM(block, jnp.bfloat16),
            pltpu.VMEM(block, jnp.bfloat16),
            dma((4,)),
            dma,
            dma,
            dma((ring - 1,)),
            dma((ring - 1,)),
            dma((ring - 1,)),
            dma((ring - 1,)),
            dma((ring, 2)),
            dma((ring, 2)),
            dma((ring, 2)),
        ],
        compiler_params=pltpu.CompilerParams(
            collective_id=0, has_side_effects=True, vmem_limit_bytes=56 << 20
        ),
        name="gather_multiply",
    )(enc_rows, weight)


def place_kernel(lengths, slot_of, order, kv_hbm, out_ref, windows, begins, request, sems):
    slot_count = lengths.shape[0]
    step, steps = pl.program_id(0), pl.num_programs(0)
    window = windows.shape[2]
    first = lax.axis_index("pool") * steps

    def lookup(s):
        who = request[first + s]
        begin = begins[who]
        base = jnp.minimum((begin // 16) * 16, kv_hbm.shape[1] - window)
        return lengths[who], begin, pl.multiple_of(base, 16)

    def fetch(s):
        base = lookup(s)[2]
        return pltpu.make_async_copy(
            kv_hbm.at[:, pl.ds(base, window), :], windows.at[s], sems.at[s]
        )

    @pl.when(step == 0)
    def _():
        def one(i, begin):
            begins[order[i]] = begin
            request[slot_of[i]] = i
            return begin + lengths[order[i]]

        lax.fori_loop(0, slot_count, one, jnp.int32(0))

        @pl.loop(0, steps)
        def _(s):
            fetch(s).start()

    size, begin, base = lookup(step)
    shape = (MAXLEN, window)
    position = lax.broadcasted_iota(jnp.int32, shape, 0)
    source = lax.broadcasted_iota(jnp.int32, shape, 1)
    chosen = (source == position + (begin - base)) & (position < size)
    picked = jnp.where(chosen, 1.0, 0.0).astype(jnp.bfloat16)
    fetch(step).wait()
    taken = [
        jnp.dot(picked, windows[step, c], preferred_element_type=jnp.float32).astype(jnp.bfloat16)
        for c in range(2)
    ]
    out_ref[0, 0] = jnp.concatenate(taken, axis=1).reshape(out_ref.shape[2:])


def place_slots(key_value, lengths, slot_of, order, half_slots):
    head_width = key_value.shape[2]
    slot_count = lengths.shape[0]
    smem = pl.BlockSpec(memory_space=pltpu.SMEM)
    shape = (1, half_slots, MAXLEN, 2, head_width)
    return pl.pallas_call(
        place_kernel,
        grid=(half_slots,),
        out_shape=jax.ShapeDtypeStruct(shape, jnp.bfloat16),
        in_specs=[smem, smem, smem, pl.BlockSpec(memory_space=pl.ANY)],
        out_specs=pl.BlockSpec((1, 1, MAXLEN, 2, head_width), lambda s: (0, s, 0, 0, 0)),
        scratch_shapes=[
            pltpu.VMEM((half_slots, 2, MAXLEN + 16, head_width), jnp.bfloat16),
            pltpu.SMEM((slot_count,), jnp.int32),
            pltpu.SMEM((slot_count,), jnp.int32),
            pltpu.SemaphoreType.DMA((half_slots,)),
        ],
        compiler_params=pltpu.CompilerParams(vmem_limit_bytes=32 << 20),
        name="place_slots",
    )(lengths, slot_of, order, key_value)


def per_device(enc_rows, kv_weight, lengths, slot_of, order):
    half_slots = lengths.shape[0] // lax.axis_size("pool")
    head_width = kv_weight.shape[3]
    mp_size = lax.axis_size("mp")
    ring_fits = (
        lax.axis_size("layer") == 2
        and lax.axis_size("pool") == 2
        and 2 <= mp_size <= 8
        and enc_rows.shape[0] % 16 == 0
        and head_width % 128 == 0
    )
    if ring_fits:
        key_value = key_values(enc_rows, kv_weight[0], mp_size)
        return place_slots(key_value, lengths, slot_of, order, half_slots)
    slot_begin, slot_size = pack_tables(lengths, slot_of, order)
    row_block = enc_rows.astype(jnp.bfloat16)
    weight = lax.all_gather(kv_weight[0], "pool", axis=0, tiled=True)
    flat_weight = weight.reshape(weight.shape[0], 2 * head_width)
    key_value = jnp.dot(
        lax.all_gather(row_block, ("mp", "layer", "pool"), axis=0, tiled=True),
        flat_weight,
        preferred_element_type=jnp.float32,
    ).astype(jnp.bfloat16)
    own_slots = lax.axis_index("pool") * (half_slots * MAXLEN) + lax.iota(
        jnp.int32, half_slots * MAXLEN
    )
    placed = place_rows(key_value, own_slots, slot_begin, slot_size)
    return placed.reshape(1, half_slots, MAXLEN, 2, head_width)


def solution(mesh):
    return jax.shard_map(
        per_device,
        mesh=mesh,
        in_specs=(
            P(("groups", "mp", "layer", "pool"), None),
            P("layer", "pool", None, "mp"),
            P("groups"),
            P("groups"),
            P("groups"),
        ),
        out_specs=P("layer", ("groups", "pool"), None, None, "mp"),
        check_vma=False,
    )
```

```python
import functools

import jax
import jax.numpy as jnp
from jax import lax
from jax.experimental import pallas as pl
from jax.experimental.pallas import tpu as pltpu
from jax.sharding import PartitionSpec as P
MAXLEN = 128


def pack_tables(lengths, slot_of, order):
    count_all = lengths.shape[0]
    request_ids = lax.iota(jnp.int32, count_all)
    selector = (order[:, None] == request_ids[None, :]).astype(jnp.int32)
    order_length = jnp.sum(selector * lengths[None, :], axis=1)
    order_begin = jnp.cumsum(order_length) - order_length
    begins = jnp.sum(selector * order_begin[:, None], axis=0)
    owner = (slot_of[:, None] == request_ids[None, :]).astype(jnp.int32)
    request = jnp.sum(owner * request_ids[:, None], axis=0)
    chooser = (request[:, None] == request_ids[None, :]).astype(jnp.int32)
    slot_begin = jnp.sum(chooser * begins[None, :], axis=1)
    slot_size = jnp.sum(chooser * lengths[None, :], axis=1)
    return (slot_begin, slot_size)


def place_rows(values, positions, slot_begin, slot_size):
    slot_count = slot_begin.shape[0]
    slot_index = positions // MAXLEN
    offset = positions % MAXLEN
    selector = (slot_index[:, None] == lax.iota(jnp.int32, slot_count)[None, :]).astype(jnp.int32)
    first_row = jnp.sum(selector * slot_begin[None, :], axis=1)
    row_limit = jnp.sum(selector * slot_size[None, :], axis=1)
    inside = offset < row_limit
    source = jnp.where(inside, first_row + offset, 0)
    taken = jnp.take(values, source, axis=0)
    return jnp.where(inside[:, None], taken, jnp.zeros((), values.dtype))


def gather_multiply(mp_size, x_ref, w_hbm, kv_hbm, w_raw, w_flat, x_send, rows, acc, part, other, done, *sems):
    w_sem, x_ss, x_rs, r_ss, r_rs, l_ss, l_rs, p_ss, p_rs, o_sem = sems
    mesh_id = pl.DeviceIdType.MESH
    ring = 2 * mp_size
    count, half = x_send.shape
    width = w_flat.shape[1]
    pool = lax.axis_index("pool")
    layer = lax.axis_index("layer")
    mp = lax.axis_index("mp")
    here = mp + layer * (ring - 1 - 2 * mp)

    def place(steps):
        at = (here + steps + ring) % ring
        on_layer = at // mp_size
        return at + on_layer * (ring - 1 - 2 * at), on_layer

    def chip(steps):
        on_mp, on_layer = place(steps)
        return on_mp * 2 + on_layer

    def device(steps):
        on_mp, on_layer = place(steps)
        return {"mp": on_mp, "layer": on_layer}

    partner = {"pool": 1 - pool}
    depth = half // 4

    def weight_copy(i):
        return pltpu.make_async_copy(
            w_hbm.at[pl.ds(i * depth, depth)], w_raw.at[pl.ds(i * depth, depth)], w_sem.at[i]
        )

    for i in range(4):
        weight_copy(i).start()
    barrier = pltpu.get_barrier_semaphore()
    for target in (device(1), device(-1), partner):
        pl.semaphore_signal(barrier, inc=1, device_id=target, device_id_type=mesh_id)
    mine = chip(0)
    rows[mine, pool] = x_ref[:, pl.ds(pl.multiple_of(pool * half, half), half)].astype(jnp.bfloat16)
    x_send[...] = x_ref[:, pl.ds(pl.multiple_of((1 - pool) * half, half), half)].astype(jnp.bfloat16)
    pl.semaphore_wait(barrier, 3)

    def send(k, direction):
        last = k == ring - 2
        second = (k % 2 == 1) or (last and direction < 0)
        core = 1 - pool if second else pool
        slot = rows.at[chip(-direction * (k // 2)), core]
        ss, rs = (r_ss, r_rs) if direction > 0 else (l_ss, l_rs)
        return pltpu.make_async_remote_copy(
            src_ref=slot, dst_ref=slot, send_sem=ss.at[k], recv_sem=rs.at[k],
            device_id=device(direction), device_id_type=mesh_id,
        )

    def swap_rows():
        return pltpu.make_async_remote_copy(
            src_ref=x_send, dst_ref=rows.at[mine, pool], send_sem=x_ss, recv_sem=x_rs,
            device_id=partner, device_id_type=mesh_id,
        )

    def arrived(k, direction):
        last = k == ring - 2
        second = (k % 2 == 1) or (last and direction < 0)
        core = 1 - pool if second else pool
        slot = rows.at[chip(-direction * (k // 2 + 1)), core]
        ss, rs = (r_ss, r_rs) if direction > 0 else (l_ss, l_rs)
        pltpu.make_async_remote_copy(
            src_ref=slot, dst_ref=slot, send_sem=ss.at[k], recv_sem=rs.at[k],
            device_id=device(direction), device_id_type=mesh_id,
        ).wait_recv()

    def flatten(i):
        weight_copy(i).wait()
        piece = 32

        @pl.loop(0, depth // piece)
        def _(t):
            start = pl.multiple_of(i * depth + t * piece, piece)
            w_flat[pl.ds(start, piece), :] = w_raw[pl.ds(start, piece)].reshape(piece, width)

    def swap_part(m, at, side):
        return pltpu.make_async_remote_copy(
            src_ref=part.at[at, side], dst_ref=other.at[at, side],
            send_sem=p_ss.at[m, side], recv_sem=p_rs.at[m, side],
            device_id=partner, device_id_type=mesh_id,
        )

    def store(m, at):
        rows_at = pl.ds(pl.multiple_of(at * 2 * count, 2 * count), 2 * count)
        return pltpu.make_async_copy(done.at[at], kv_hbm.at[rows_at], o_sem.at[m])

    side_width = width // 2
    columns = 256 if side_width % 256 == 0 else 128

    def multiply(chips, m):
        for side in range(2):

            @pl.loop(0, side_width // columns)
            def _(t):
                start = pl.multiple_of(t * columns, columns)
                span = pl.ds(start, columns)
                wide = pl.ds(pl.multiple_of(side * side_width + start, columns), columns)
                left = jnp.concatenate([rows[c].reshape(2 * count, half) for c in chips], axis=0)
                product = jnp.dot(left, w_flat[:, wide], preferred_element_type=jnp.float32)
                for i, c in enumerate(chips):
                    one = product[i * 2 * count : (i + 1) * 2 * count]
                    acc[c, side, :, span] = one
                    part[c, side, :, span] = one.astype(jnp.bfloat16)

            for i, c in enumerate(chips):
                swap_part(m + i, c, side).start()

    def finish(chips, m):
        piece = 16
        for i, c in enumerate(chips):
            for side in range(2):
                swap_part(m + i, c, side).wait_recv()

            @pl.loop(0, 2 * count // piece)
            def _(t):
                span = pl.ds(pl.multiple_of(t * piece, piece), piece)
                total = [
                    (acc[c, side, span, :] + other[c, side, span, :].astype(jnp.float32)).astype(jnp.bfloat16)
                    for side in range(2)
                ]
                done[c, span] = jnp.concatenate(total, axis=1).reshape(piece, 2, side_width)

            store(m + i, c).start()

    send(0, 1).start()
    send(0, -1).start()
    swap_rows().start()
    swap_rows().wait_recv()
    send(1, 1).start()
    send(1, -1).start()
    flatten(0)
    flatten(1)
    reach = ring // 2
    waiting = None
    for k in range(ring - 1):
        if k == ring - 2:
            finish(*waiting)
        ahead = k + 2
        arrived(k, 1)
        if ahead <= ring - 2:
            send(ahead, 1).start()
        arrived(k, -1)
        if ahead < ring - 2:
            send(ahead, -1).start()
        elif ahead == ring - 1:
            send(ring - 2, -1).start()
        if k == 0:
            flatten(2)
            flatten(3)
            multiply([mine], 0)
            waiting = ([mine], 0)
        elif k % 2 == 1:
            d = (k + 1) // 2
            chips = [chip(-d), chip(d)]
            if d == 1:
                finish(*waiting)
            multiply(chips, 2 * d - 1)
            waiting = (chips, 2 * d - 1)
        elif k < ring - 2:
            finish(*waiting)
    multiply([chip(reach)], ring - 1)
    finish([chip(reach)], ring - 1)
    swap_rows().wait_send()
    for k in range(ring - 1):
        send(k, 1).wait_send()
        send(k, -1).wait_send()
    blocks = [mine]
    for d in range(1, reach):
        blocks += [chip(-d), chip(d)]
    for m, c in enumerate(blocks + [chip(reach)]):
        for side in range(2):
            swap_part(m, c, side).wait_send()
        store(m, c).wait()


def key_values(enc_rows, weight, mp_size):
    count, features = enc_rows.shape
    half, _, head_width = weight.shape
    width, ring = 2 * head_width, 2 * mp_size
    dma = pltpu.SemaphoreType.DMA
    block = (ring, 2, 2 * count, head_width)
    return pl.pallas_call(
        functools.partial(gather_multiply, mp_size),
        out_shape=jax.ShapeDtypeStruct((ring * 2 * count, 2, head_width), jnp.bfloat16),
        in_specs=[pl.BlockSpec(memory_space=pltpu.VMEM), pl.BlockSpec(memory_space=pl.ANY)],
        out_specs=pl.BlockSpec(memory_space=pl.ANY),
        scratch_shapes=[
            pltpu.VMEM(weight.shape, jnp.bfloat16),
            pltpu.VMEM((half, width), jnp.bfloat16),
            pltpu.VMEM((count, half), jnp.bfloat16),
            pltpu.VMEM((ring, 2, count, half), jnp.bfloat16),
            pltpu.VMEM(block, jnp.float32),
            pltpu.VMEM(block, jnp.bfloat16),
            pltpu.VMEM(block, jnp.bfloat16),
            pltpu.VMEM((ring, 2 * count, 2, head_width), jnp.bfloat16),
            dma((4,)),
            dma,
            dma,
            dma((ring - 1,)),
            dma((ring - 1,)),
            dma((ring - 1,)),
            dma((ring - 1,)),
            dma((ring, 2)),
            dma((ring, 2)),
            dma((ring,)),
        ],
        compiler_params=pltpu.CompilerParams(
            collective_id=0, has_side_effects=True, vmem_limit_bytes=56 << 20
        ),
        name="gather_multiply",
    )(enc_rows, weight)


def place_kernel(lengths, slot_of, order, kv_hbm, out_hbm, windows, begins, request, in_sems, out_sems):
    slot_count = lengths.shape[0]
    half_slots = windows.shape[0]
    first = lax.axis_index("pool") * half_slots

    def one(i, begin):
        begins[order[i]] = begin
        request[slot_of[i]] = i
        return begin + lengths[order[i]]

    lax.fori_loop(0, slot_count, one, jnp.int32(0))

    def lookup(s):
        who = request[first + s]
        base = jnp.minimum(begins[who], kv_hbm.shape[0] - MAXLEN)
        return lengths[who], base, begins[who] - base

    def fetch(s):
        base = lookup(s)[1]
        return pltpu.make_async_copy(
            kv_hbm.at[pl.ds(base, MAXLEN)], windows.at[s, pl.ds(0, MAXLEN)], in_sems.at[s]
        )

    def write(s):
        skip = lookup(s)[2]
        return pltpu.make_async_copy(
            windows.at[s, pl.ds(skip, MAXLEN)], out_hbm.at[0, s], out_sems.at[s]
        )

    for s in range(half_slots):
        fetch(s).start()
    blank = jnp.zeros(windows.shape[2:], windows.dtype)
    for s in range(half_slots):
        size, _, skip = lookup(s)
        fetch(s).wait()

        @pl.loop(skip + size, skip + MAXLEN)
        def _(j):
            windows[s, j] = blank

        write(s).start()
    for s in range(half_slots):
        write(s).wait()


def place_slots(key_value, lengths, slot_of, order, half_slots):
    head_width = key_value.shape[2]
    slot_count = lengths.shape[0]
    smem = pl.BlockSpec(memory_space=pltpu.SMEM)
    shape = (1, half_slots, MAXLEN, 2, head_width)
    return pl.pallas_call(
        place_kernel,
        out_shape=jax.ShapeDtypeStruct(shape, jnp.bfloat16),
        in_specs=[smem, smem, smem, pl.BlockSpec(memory_space=pl.ANY)],
        out_specs=pl.BlockSpec(memory_space=pl.ANY),
        scratch_shapes=[
            pltpu.VMEM((half_slots, 2 * MAXLEN, 2, head_width), jnp.bfloat16),
            pltpu.SMEM((slot_count,), jnp.int32),
            pltpu.SMEM((slot_count,), jnp.int32),
            pltpu.SemaphoreType.DMA((half_slots,)),
            pltpu.SemaphoreType.DMA((half_slots,)),
        ],
        compiler_params=pltpu.CompilerParams(vmem_limit_bytes=56 << 20),
        name="place_slots",
    )(lengths, slot_of, order, key_value)


def per_device(enc_rows, kv_weight, lengths, slot_of, order):
    half_slots = lengths.shape[0] // lax.axis_size("pool")
    head_width = kv_weight.shape[3]
    mp_size = lax.axis_size("mp")
    ring_fits = (
        lax.axis_size("layer") == 2
        and lax.axis_size("pool") == 2
        and 2 <= mp_size <= 8
        and enc_rows.shape[0] % 16 == 0
        and head_width % 128 == 0
    )
    if ring_fits:
        key_value = key_values(enc_rows, kv_weight[0], mp_size)
        return place_slots(key_value, lengths, slot_of, order, half_slots)
    slot_begin, slot_size = pack_tables(lengths, slot_of, order)
    row_block = enc_rows.astype(jnp.bfloat16)
    weight = lax.all_gather(kv_weight[0], "pool", axis=0, tiled=True)
    flat_weight = weight.reshape(weight.shape[0], 2 * head_width)
    key_value = jnp.dot(
        lax.all_gather(row_block, ("mp", "layer", "pool"), axis=0, tiled=True),
        flat_weight,
        preferred_element_type=jnp.float32,
    ).astype(jnp.bfloat16)
    own_slots = lax.axis_index("pool") * (half_slots * MAXLEN) + lax.iota(
        jnp.int32, half_slots * MAXLEN
    )
    placed = place_rows(key_value, own_slots, slot_begin, slot_size)
    return placed.reshape(1, half_slots, MAXLEN, 2, head_width)


def solution(mesh):
    return jax.shard_map(
        per_device,
        mesh=mesh,
        in_specs=(
            P(("groups", "mp", "layer", "pool"), None),
            P("layer", "pool", None, "mp"),
            P("groups"),
            P("groups"),
            P("groups"),
        ),
        out_specs=P("layer", ("groups", "pool"), None, None, "mp"),
        check_vma=False,
    )
```

```python
import functools

import jax
import jax.numpy as jnp
from jax import lax
from jax.experimental import pallas as pl
from jax.experimental.pallas import tpu as pltpu
from jax.sharding import PartitionSpec as P
MAXLEN = 128
BLANK = 16


def pack_tables(lengths, slot_of, order):
    count_all = lengths.shape[0]
    request_ids = lax.iota(jnp.int32, count_all)
    selector = (order[:, None] == request_ids[None, :]).astype(jnp.int32)
    order_length = jnp.sum(selector * lengths[None, :], axis=1)
    order_begin = jnp.cumsum(order_length) - order_length
    begins = jnp.sum(selector * order_begin[:, None], axis=0)
    owner = (slot_of[:, None] == request_ids[None, :]).astype(jnp.int32)
    request = jnp.sum(owner * request_ids[:, None], axis=0)
    chooser = (request[:, None] == request_ids[None, :]).astype(jnp.int32)
    slot_begin = jnp.sum(chooser * begins[None, :], axis=1)
    slot_size = jnp.sum(chooser * lengths[None, :], axis=1)
    return (slot_begin, slot_size)


def place_rows(values, positions, slot_begin, slot_size):
    slot_count = slot_begin.shape[0]
    slot_index = positions // MAXLEN
    offset = positions % MAXLEN
    selector = (slot_index[:, None] == lax.iota(jnp.int32, slot_count)[None, :]).astype(jnp.int32)
    first_row = jnp.sum(selector * slot_begin[None, :], axis=1)
    row_limit = jnp.sum(selector * slot_size[None, :], axis=1)
    inside = offset < row_limit
    source = jnp.where(inside, first_row + offset, 0)
    taken = jnp.take(values, source, axis=0)
    return jnp.where(inside[:, None], taken, jnp.zeros((), values.dtype))


def gather_multiply(mp_size, x_ref, w_hbm, kv_hbm, w_raw, w_flat, x_send, rows, acc, part, other, done, *sems):
    w_sem, x_ss, x_rs, r_ss, r_rs, l_ss, l_rs, p_ss, p_rs, o_sem = sems
    mesh_id = pl.DeviceIdType.MESH
    ring = 2 * mp_size
    count, half = x_send.shape
    width = w_flat.shape[1]
    pool = lax.axis_index("pool")
    layer = lax.axis_index("layer")
    mp = lax.axis_index("mp")
    here = mp + layer * (ring - 1 - 2 * mp)

    def place(steps):
        at = (here + steps + ring) % ring
        on_layer = at // mp_size
        return at + on_layer * (ring - 1 - 2 * at), on_layer

    def chip(steps):
        on_mp, on_layer = place(steps)
        return on_mp * 2 + on_layer

    def device(steps):
        on_mp, on_layer = place(steps)
        return {"mp": on_mp, "layer": on_layer}

    partner = {"pool": 1 - pool}
    depth = half // 4

    def weight_copy(i):
        return pltpu.make_async_copy(
            w_hbm.at[pl.ds(i * depth, depth)], w_raw.at[pl.ds(i * depth, depth)], w_sem.at[i]
        )

    for i in range(4):
        weight_copy(i).start()
    barrier = pltpu.get_barrier_semaphore()
    for target in (device(1), device(-1), partner):
        pl.semaphore_signal(barrier, inc=1, device_id=target, device_id_type=mesh_id)
    mine = chip(0)
    rows[mine, pool] = x_ref[:, pl.ds(pl.multiple_of(pool * half, half), half)].astype(jnp.bfloat16)
    pl.semaphore_wait(barrier, 3)

    def ring_copy(k, direction, hops):
        step = min(k, ring - 2)
        second = (k % 2 == 1) if k < ring - 2 else direction < 0
        slot = rows.at[chip(-direction * (step // 2 + hops)), 1 - pool if second else pool]
        if k >= ring - 2:
            slot = slot.at[:, pl.ds((k - step) * (half // 2), half // 2)]
        ss, rs = (r_ss, r_rs) if direction > 0 else (l_ss, l_rs)
        return pltpu.make_async_remote_copy(
            src_ref=slot, dst_ref=slot, send_sem=ss.at[k], recv_sem=rs.at[k],
            device_id=device(direction), device_id_type=mesh_id,
        )

    def send(k, direction):
        return ring_copy(k, direction, 0)

    def arrived(k, direction):
        ring_copy(k, direction, 1).wait_recv()

    def swap_rows():
        return pltpu.make_async_remote_copy(
            src_ref=x_send, dst_ref=rows.at[mine, pool], send_sem=x_ss, recv_sem=x_rs,
            device_id=partner, device_id_type=mesh_id,
        )

    def flatten(i):
        weight_copy(i).wait()
        piece = 32

        @pl.loop(0, depth // piece)
        def _(t):
            start = pl.multiple_of(i * depth + t * piece, piece)
            w_flat[pl.ds(start, piece), :] = w_raw[pl.ds(start, piece)].reshape(piece, width)

    def swap_part(m, at, side):
        return pltpu.make_async_remote_copy(
            src_ref=part.at[at, side], dst_ref=other.at[at, side],
            send_sem=p_ss.at[m, side], recv_sem=p_rs.at[m, side],
            device_id=partner, device_id_type=mesh_id,
        )

    def store(m, at):
        rows_at = pl.ds(pl.multiple_of(at * 2 * count, 2 * count), 2 * count)
        return pltpu.make_async_copy(done.at[at], kv_hbm.at[rows_at], o_sem.at[m])

    side_width = width // 2
    columns = 256 if side_width % 256 == 0 else 128

    def multiply(chips, m, begin=0, size=half, is_last=True):
        for side in range(2):

            @pl.loop(0, side_width // columns)
            def _(t):
                start = pl.multiple_of(t * columns, columns)
                span = pl.ds(start, columns)
                wide = pl.ds(pl.multiple_of(side * side_width + start, columns), columns)
                left = jnp.concatenate(
                    [rows[c, :, :, begin : begin + size].reshape(2 * count, size) for c in chips],
                    axis=0,
                )
                product = jnp.dot(
                    left, w_flat[begin : begin + size, wide], preferred_element_type=jnp.float32
                )
                for i, c in enumerate(chips):
                    one = product[i * 2 * count : (i + 1) * 2 * count]
                    if begin > 0:
                        one = one + acc[c, side, :, span]
                    acc[c, side, :, span] = one
                    if is_last:
                        part[c, side, :, span] = one.astype(jnp.bfloat16)

            if is_last:
                for i, c in enumerate(chips):
                    swap_part(m + i, c, side).start()

    def finish(chips, m):
        piece = 16
        for i, c in enumerate(chips):
            for side in range(2):
                swap_part(m + i, c, side).wait_recv()

            @pl.loop(0, 2 * count // piece)
            def _(t):
                span = pl.ds(pl.multiple_of(t * piece, piece), piece)
                total = [
                    (acc[c, side, span, :] + other[c, side, span, :].astype(jnp.float32)).astype(jnp.bfloat16)
                    for side in range(2)
                ]
                done[c, span] = jnp.concatenate(total, axis=1).reshape(piece, 2, side_width)

            store(m + i, c).start()

    send(0, 1).start()
    send(0, -1).start()
    x_send[...] = x_ref[:, pl.ds(pl.multiple_of((1 - pool) * half, half), half)].astype(jnp.bfloat16)
    swap_rows().start()
    swap_rows().wait_recv()
    send(1, 1).start()
    send(1, -1).start()
    flatten(0)
    flatten(1)
    reach = ring // 2
    waiting = None
    for k in range(ring - 2):
        ahead = k + 2
        arrived(k, 1)
        if ahead <= ring - 2:
            send(ahead, 1).start()
        if ahead == ring - 2:
            send(ring - 1, 1).start()
        arrived(k, -1)
        if ahead < ring - 2:
            send(ahead, -1).start()
        elif ahead == ring - 1:
            send(ring - 2, -1).start()
            send(ring - 1, -1).start()
        if k == 0:
            flatten(2)
            flatten(3)
            multiply([mine], 0)
            waiting = ([mine], 0)
        elif k % 2 == 1:
            d = (k + 1) // 2
            chips = [chip(-d), chip(d)]
            if d == 1:
                finish(*waiting)
            multiply(chips, 2 * d - 1)
            waiting = (chips, 2 * d - 1)
        else:
            finish(*waiting)
    finish(*waiting)
    for part_of in range(2):
        arrived(ring - 2 + part_of, 1)
        arrived(ring - 2 + part_of, -1)
        multiply([chip(reach)], ring - 1, part_of * (half // 2), half // 2, part_of == 1)
    finish([chip(reach)], ring - 1)
    swap_rows().wait_send()
    for k in range(ring):
        send(k, 1).wait_send()
        send(k, -1).wait_send()
    blocks = [mine]
    for d in range(1, reach):
        blocks += [chip(-d), chip(d)]
    for m, c in enumerate(blocks + [chip(reach)]):
        for side in range(2):
            swap_part(m, c, side).wait_send()
        store(m, c).wait()


def key_values(enc_rows, weight, mp_size):
    count, features = enc_rows.shape
    half, _, head_width = weight.shape
    width, ring = 2 * head_width, 2 * mp_size
    dma = pltpu.SemaphoreType.DMA
    block = (ring, 2, 2 * count, head_width)
    return pl.pallas_call(
        functools.partial(gather_multiply, mp_size),
        out_shape=jax.ShapeDtypeStruct((ring * 2 * count, 2, head_width), jnp.bfloat16),
        in_specs=[pl.BlockSpec(memory_space=pltpu.VMEM), pl.BlockSpec(memory_space=pl.ANY)],
        out_specs=pl.BlockSpec(memory_space=pl.ANY),
        scratch_shapes=[
            pltpu.VMEM(weight.shape, jnp.bfloat16),
            pltpu.VMEM((half, width), jnp.bfloat16),
            pltpu.VMEM((count, half), jnp.bfloat16),
            pltpu.VMEM((ring, 2, count, half), jnp.bfloat16),
            pltpu.VMEM(block, jnp.float32),
            pltpu.VMEM(block, jnp.bfloat16),
            pltpu.VMEM(block, jnp.bfloat16),
            pltpu.VMEM((ring, 2 * count, 2, head_width), jnp.bfloat16),
            dma((4,)),
            dma,
            dma,
            dma((ring,)),
            dma((ring,)),
            dma((ring,)),
            dma((ring,)),
            dma((ring, 2)),
            dma((ring, 2)),
            dma((ring,)),
        ],
        compiler_params=pltpu.CompilerParams(
            collective_id=0, has_side_effects=True, vmem_limit_bytes=56 << 20
        ),
        name="gather_multiply",
    )(enc_rows, weight)


def place_kernel(lengths, slot_of, order, kv_hbm, out_hbm, windows, begins, request, in_sems, out_sems):
    slot_count = lengths.shape[0]
    half_slots = windows.shape[0]
    first = lax.axis_index("pool") * half_slots

    def one(i, begin):
        begins[order[i]] = begin
        request[slot_of[i]] = i
        return begin + lengths[order[i]]

    lax.fori_loop(0, slot_count, one, jnp.int32(0))

    def lookup(s):
        who = request[first + s]
        base = jnp.minimum(begins[who], kv_hbm.shape[0] - MAXLEN)
        return lengths[who], base, begins[who] - base

    def fetch(s):
        base = lookup(s)[1]
        return pltpu.make_async_copy(
            kv_hbm.at[pl.ds(base, MAXLEN)], windows.at[s, pl.ds(0, MAXLEN)], in_sems.at[s]
        )

    def write(s):
        skip = lookup(s)[2]
        return pltpu.make_async_copy(
            windows.at[s, pl.ds(skip, MAXLEN)], out_hbm.at[0, s], out_sems.at[s]
        )

    for s in range(half_slots):
        fetch(s).start()
    blank = jnp.zeros((BLANK, *windows.shape[2:]), windows.dtype)
    for s in range(half_slots):
        size, _, skip = lookup(s)
        fetch(s).wait()

        @pl.loop(0, (MAXLEN - size + BLANK - 1) // BLANK)
        def _(j):
            windows[s, pl.ds(skip + size + j * BLANK, BLANK)] = blank

        write(s).start()
    for s in range(half_slots):
        write(s).wait()


def place_slots(key_value, lengths, slot_of, order, half_slots):
    head_width = key_value.shape[2]
    slot_count = lengths.shape[0]
    smem = pl.BlockSpec(memory_space=pltpu.SMEM)
    shape = (1, half_slots, MAXLEN, 2, head_width)
    return pl.pallas_call(
        place_kernel,
        out_shape=jax.ShapeDtypeStruct(shape, jnp.bfloat16),
        in_specs=[smem, smem, smem, pl.BlockSpec(memory_space=pl.ANY)],
        out_specs=pl.BlockSpec(memory_space=pl.ANY),
        scratch_shapes=[
            pltpu.VMEM((half_slots, 2 * MAXLEN + BLANK, 2, head_width), jnp.bfloat16),
            pltpu.SMEM((slot_count,), jnp.int32),
            pltpu.SMEM((slot_count,), jnp.int32),
            pltpu.SemaphoreType.DMA((half_slots,)),
            pltpu.SemaphoreType.DMA((half_slots,)),
        ],
        compiler_params=pltpu.CompilerParams(vmem_limit_bytes=56 << 20),
        name="place_slots",
    )(lengths, slot_of, order, key_value)


def per_device(enc_rows, kv_weight, lengths, slot_of, order):
    half_slots = lengths.shape[0] // lax.axis_size("pool")
    head_width = kv_weight.shape[3]
    mp_size = lax.axis_size("mp")
    ring_fits = (
        lax.axis_size("layer") == 2
        and lax.axis_size("pool") == 2
        and 2 <= mp_size <= 8
        and enc_rows.shape[0] % 16 == 0
        and head_width % 128 == 0
        and kv_weight.shape[1] % 256 == 0
    )
    if ring_fits:
        key_value = key_values(enc_rows, kv_weight[0], mp_size)
        return place_slots(key_value, lengths, slot_of, order, half_slots)
    slot_begin, slot_size = pack_tables(lengths, slot_of, order)
    row_block = enc_rows.astype(jnp.bfloat16)
    weight = lax.all_gather(kv_weight[0], "pool", axis=0, tiled=True)
    flat_weight = weight.reshape(weight.shape[0], 2 * head_width)
    key_value = jnp.dot(
        lax.all_gather(row_block, ("mp", "layer", "pool"), axis=0, tiled=True),
        flat_weight,
        preferred_element_type=jnp.float32,
    ).astype(jnp.bfloat16)
    own_slots = lax.axis_index("pool") * (half_slots * MAXLEN) + lax.iota(
        jnp.int32, half_slots * MAXLEN
    )
    placed = place_rows(key_value, own_slots, slot_begin, slot_size)
    return placed.reshape(1, half_slots, MAXLEN, 2, head_width)


def solution(mesh):
    return jax.shard_map(
        per_device,
        mesh=mesh,
        in_specs=(
            P(("groups", "mp", "layer", "pool"), None),
            P("layer", "pool", None, "mp"),
            P("groups"),
            P("groups"),
            P("groups"),
        ),
        out_specs=P("layer", ("groups", "pool"), None, None, "mp"),
        check_vma=False,
    )
```

```python
import functools

import jax
import jax.numpy as jnp
from jax import lax
from jax.experimental import pallas as pl
from jax.experimental.pallas import tpu as pltpu
from jax.sharding import PartitionSpec as P
MAXLEN = 128
BLANK = 16


def pack_tables(lengths, slot_of, order):
    count_all = lengths.shape[0]
    request_ids = lax.iota(jnp.int32, count_all)
    selector = (order[:, None] == request_ids[None, :]).astype(jnp.int32)
    order_length = jnp.sum(selector * lengths[None, :], axis=1)
    order_begin = jnp.cumsum(order_length) - order_length
    begins = jnp.sum(selector * order_begin[:, None], axis=0)
    owner = (slot_of[:, None] == request_ids[None, :]).astype(jnp.int32)
    request = jnp.sum(owner * request_ids[:, None], axis=0)
    chooser = (request[:, None] == request_ids[None, :]).astype(jnp.int32)
    slot_begin = jnp.sum(chooser * begins[None, :], axis=1)
    slot_size = jnp.sum(chooser * lengths[None, :], axis=1)
    return (slot_begin, slot_size)


def place_rows(values, positions, slot_begin, slot_size):
    slot_count = slot_begin.shape[0]
    slot_index = positions // MAXLEN
    offset = positions % MAXLEN
    selector = (slot_index[:, None] == lax.iota(jnp.int32, slot_count)[None, :]).astype(jnp.int32)
    first_row = jnp.sum(selector * slot_begin[None, :], axis=1)
    row_limit = jnp.sum(selector * slot_size[None, :], axis=1)
    inside = offset < row_limit
    source = jnp.where(inside, first_row + offset, 0)
    taken = jnp.take(values, source, axis=0)
    return jnp.where(inside[:, None], taken, jnp.zeros((), values.dtype))


def gather_multiply(mp_size, x_ref, w_hbm, kv_hbm, w_raw, w_flat, x_send, rows, acc, part, other, done, *sems):
    w_sem, x_ss, x_rs, r_ss, r_rs, l_ss, l_rs, p_ss, p_rs, o_sem = sems
    mesh_id = pl.DeviceIdType.MESH
    ring = 2 * mp_size
    count, half = x_send.shape
    width = w_flat.shape[1]
    pool = lax.axis_index("pool")
    layer = lax.axis_index("layer")
    mp = lax.axis_index("mp")
    here = mp + layer * (ring - 1 - 2 * mp)

    def place(steps):
        at = (here + steps + ring) % ring
        on_layer = at // mp_size
        return at + on_layer * (ring - 1 - 2 * at), on_layer

    def chip(steps):
        on_mp, on_layer = place(steps)
        return on_mp * 2 + on_layer

    def device(steps):
        on_mp, on_layer = place(steps)
        return {"mp": on_mp, "layer": on_layer}

    partner = {"pool": 1 - pool}
    depth = half // 4

    def weight_copy(i):
        return pltpu.make_async_copy(
            w_hbm.at[pl.ds(i * depth, depth)], w_raw.at[pl.ds(i * depth, depth)], w_sem.at[i]
        )

    for i in range(4):
        weight_copy(i).start()
    barrier = pltpu.get_barrier_semaphore()
    for target in (device(1), device(-1), partner):
        pl.semaphore_signal(barrier, inc=1, device_id=target, device_id_type=mesh_id)
    mine = chip(0)
    rows[mine, pool] = x_ref[:, pl.ds(pl.multiple_of(pool * half, half), half)].astype(jnp.bfloat16)
    x_send[...] = x_ref[:, pl.ds(pl.multiple_of((1 - pool) * half, half), half)].astype(jnp.bfloat16)
    pl.semaphore_wait(barrier, 3)

    def send(k, direction):
        last = k == ring - 2
        second = (k % 2 == 1) or (last and direction < 0)
        core = 1 - pool if second else pool
        slot = rows.at[chip(-direction * (k // 2)), core]
        ss, rs = (r_ss, r_rs) if direction > 0 else (l_ss, l_rs)
        return pltpu.make_async_remote_copy(
            src_ref=slot, dst_ref=slot, send_sem=ss.at[k], recv_sem=rs.at[k],
            device_id=device(direction), device_id_type=mesh_id,
        )

    def swap_rows():
        return pltpu.make_async_remote_copy(
            src_ref=x_send, dst_ref=rows.at[mine, pool], send_sem=x_ss, recv_sem=x_rs,
            device_id=partner, device_id_type=mesh_id,
        )

    def arrived(k, direction):
        last = k == ring - 2
        second = (k % 2 == 1) or (last and direction < 0)
        core = 1 - pool if second else pool
        slot = rows.at[chip(-direction * (k // 2 + 1)), core]
        ss, rs = (r_ss, r_rs) if direction > 0 else (l_ss, l_rs)
        pltpu.make_async_remote_copy(
            src_ref=slot, dst_ref=slot, send_sem=ss.at[k], recv_sem=rs.at[k],
            device_id=device(direction), device_id_type=mesh_id,
        ).wait_recv()

    def flatten(i):
        weight_copy(i).wait()
        piece = 32

        @pl.loop(0, depth // piece)
        def _(t):
            start = pl.multiple_of(i * depth + t * piece, piece)
            w_flat[pl.ds(start, piece), :] = w_raw[pl.ds(start, piece)].reshape(piece, width)

    def swap_part(m, at, side):
        return pltpu.make_async_remote_copy(
            src_ref=part.at[at, side], dst_ref=other.at[at, side],
            send_sem=p_ss.at[m, side], recv_sem=p_rs.at[m, side],
            device_id=partner, device_id_type=mesh_id,
        )

    def store(m, at):
        rows_at = pl.ds(pl.multiple_of(at * 2 * count, 2 * count), 2 * count)
        return pltpu.make_async_copy(done.at[at], kv_hbm.at[rows_at], o_sem.at[m])

    side_width = width // 2
    columns = 512 if side_width % 512 == 0 else 128

    def multiply(chips, m):
        for side in range(2):

            @pl.loop(0, side_width // columns)
            def _(t):
                start = pl.multiple_of(t * columns, columns)
                span = pl.ds(start, columns)
                wide = pl.ds(pl.multiple_of(side * side_width + start, columns), columns)
                left = jnp.concatenate([rows[c].reshape(2 * count, half) for c in chips], axis=0)
                product = jnp.dot(left, w_flat[:, wide], preferred_element_type=jnp.float32)
                for i, c in enumerate(chips):
                    one = product[i * 2 * count : (i + 1) * 2 * count]
                    acc[c, side, :, span] = one
                    part[c, side, :, span] = one.astype(jnp.bfloat16)

            for i, c in enumerate(chips):
                swap_part(m + i, c, side).start()

    def finish(chips, m):
        piece = 16
        for i, c in enumerate(chips):
            for side in range(2):
                swap_part(m + i, c, side).wait_recv()

            @pl.loop(0, 2 * count // piece)
            def _(t):
                span = pl.ds(pl.multiple_of(t * piece, piece), piece)
                total = [
                    (acc[c, side, span, :] + other[c, side, span, :].astype(jnp.float32)).astype(jnp.bfloat16)
                    for side in range(2)
                ]
                done[c, span] = jnp.concatenate(total, axis=1).reshape(piece, 2, side_width)

            store(m + i, c).start()

    send(0, 1).start()
    send(0, -1).start()
    swap_rows().start()
    swap_rows().wait_recv()
    send(1, 1).start()
    send(1, -1).start()
    flatten(0)
    flatten(1)
    reach = ring // 2
    waiting = None
    for k in range(ring - 1):
        if k == ring - 2:
            finish(*waiting)
        ahead = k + 2
        arrived(k, 1)
        if ahead <= ring - 2:
            send(ahead, 1).start()
        arrived(k, -1)
        if ahead < ring - 2:
            send(ahead, -1).start()
        elif ahead == ring - 1:
            send(ring - 2, -1).start()
        if k == 0:
            flatten(2)
            flatten(3)
            multiply([mine], 0)
            waiting = ([mine], 0)
        elif k % 2 == 1:
            d = (k + 1) // 2
            chips = [chip(-d), chip(d)]
            if d == 1:
                finish(*waiting)
            multiply(chips, 2 * d - 1)
            waiting = (chips, 2 * d - 1)
        elif k < ring - 2:
            finish(*waiting)
    multiply([chip(reach)], ring - 1)
    finish([chip(reach)], ring - 1)
    swap_rows().wait_send()
    for k in range(ring - 1):
        send(k, 1).wait_send()
        send(k, -1).wait_send()
    blocks = [mine]
    for d in range(1, reach):
        blocks += [chip(-d), chip(d)]
    for m, c in enumerate(blocks + [chip(reach)]):
        for side in range(2):
            swap_part(m, c, side).wait_send()
        store(m, c).wait()


def key_values(enc_rows, weight, mp_size):
    count, features = enc_rows.shape
    half, _, head_width = weight.shape
    width, ring = 2 * head_width, 2 * mp_size
    dma = pltpu.SemaphoreType.DMA
    block = (ring, 2, 2 * count, head_width)
    return pl.pallas_call(
        functools.partial(gather_multiply, mp_size),
        out_shape=jax.ShapeDtypeStruct((ring * 2 * count, 2, head_width), jnp.bfloat16),
        in_specs=[pl.BlockSpec(memory_space=pltpu.VMEM), pl.BlockSpec(memory_space=pl.ANY)],
        out_specs=pl.BlockSpec(memory_space=pl.ANY),
        scratch_shapes=[
            pltpu.VMEM(weight.shape, jnp.bfloat16),
            pltpu.VMEM((half, width), jnp.bfloat16),
            pltpu.VMEM((count, half), jnp.bfloat16),
            pltpu.VMEM((ring, 2, count, half), jnp.bfloat16),
            pltpu.VMEM(block, jnp.float32),
            pltpu.VMEM(block, jnp.bfloat16),
            pltpu.VMEM(block, jnp.bfloat16),
            pltpu.VMEM((ring, 2 * count, 2, head_width), jnp.bfloat16),
            dma((4,)),
            dma,
            dma,
            dma((ring - 1,)),
            dma((ring - 1,)),
            dma((ring - 1,)),
            dma((ring - 1,)),
            dma((ring, 2)),
            dma((ring, 2)),
            dma((ring,)),
        ],
        compiler_params=pltpu.CompilerParams(
            collective_id=0, has_side_effects=True, vmem_limit_bytes=56 << 20
        ),
        name="gather_multiply",
    )(enc_rows, weight)


def place_kernel(lengths, slot_of, order, kv_hbm, out_hbm, windows, begins, request, in_sems, out_sems):
    slot_count = lengths.shape[0]
    half_slots = windows.shape[0]
    first = lax.axis_index("pool") * half_slots

    def one(i, begin):
        begins[order[i]] = begin
        request[slot_of[i]] = i
        return begin + lengths[order[i]]

    lax.fori_loop(0, slot_count, one, jnp.int32(0))

    def lookup(s):
        who = request[first + s]
        base = jnp.minimum(begins[who], kv_hbm.shape[0] - MAXLEN)
        return lengths[who], base, begins[who] - base

    def fetch(s):
        base = lookup(s)[1]
        return pltpu.make_async_copy(
            kv_hbm.at[pl.ds(base, MAXLEN)], windows.at[s, pl.ds(0, MAXLEN)], in_sems.at[s]
        )

    def write(s):
        skip = lookup(s)[2]
        return pltpu.make_async_copy(
            windows.at[s, pl.ds(skip, MAXLEN)], out_hbm.at[0, s], out_sems.at[s]
        )

    for s in range(half_slots):
        fetch(s).start()
    blank = jnp.zeros((BLANK, *windows.shape[2:]), windows.dtype)
    for s in range(half_slots):
        size, _, skip = lookup(s)
        fetch(s).wait()

        @pl.loop(0, (MAXLEN - size + BLANK - 1) // BLANK)
        def _(j):
            windows[s, pl.ds(skip + size + j * BLANK, BLANK)] = blank

        write(s).start()
    for s in range(half_slots):
        write(s).wait()


def place_slots(key_value, lengths, slot_of, order, half_slots):
    head_width = key_value.shape[2]
    slot_count = lengths.shape[0]
    smem = pl.BlockSpec(memory_space=pltpu.SMEM)
    shape = (1, half_slots, MAXLEN, 2, head_width)
    return pl.pallas_call(
        place_kernel,
        out_shape=jax.ShapeDtypeStruct(shape, jnp.bfloat16),
        in_specs=[smem, smem, smem, pl.BlockSpec(memory_space=pl.ANY)],
        out_specs=pl.BlockSpec(memory_space=pl.ANY),
        scratch_shapes=[
            pltpu.VMEM((half_slots, 2 * MAXLEN + BLANK, 2, head_width), jnp.bfloat16),
            pltpu.SMEM((slot_count,), jnp.int32),
            pltpu.SMEM((slot_count,), jnp.int32),
            pltpu.SemaphoreType.DMA((half_slots,)),
            pltpu.SemaphoreType.DMA((half_slots,)),
        ],
        compiler_params=pltpu.CompilerParams(vmem_limit_bytes=56 << 20),
        name="place_slots",
    )(lengths, slot_of, order, key_value)


def per_device(enc_rows, kv_weight, lengths, slot_of, order):
    half_slots = lengths.shape[0] // lax.axis_size("pool")
    head_width = kv_weight.shape[3]
    mp_size = lax.axis_size("mp")
    ring_fits = (
        lax.axis_size("layer") == 2
        and lax.axis_size("pool") == 2
        and 2 <= mp_size <= 8
        and enc_rows.shape[0] % 16 == 0
        and head_width % 128 == 0
    )
    if ring_fits:
        key_value = key_values(enc_rows, kv_weight[0], mp_size)
        return place_slots(key_value, lengths, slot_of, order, half_slots)
    slot_begin, slot_size = pack_tables(lengths, slot_of, order)
    row_block = enc_rows.astype(jnp.bfloat16)
    weight = lax.all_gather(kv_weight[0], "pool", axis=0, tiled=True)
    flat_weight = weight.reshape(weight.shape[0], 2 * head_width)
    key_value = jnp.dot(
        lax.all_gather(row_block, ("mp", "layer", "pool"), axis=0, tiled=True),
        flat_weight,
        preferred_element_type=jnp.float32,
    ).astype(jnp.bfloat16)
    own_slots = lax.axis_index("pool") * (half_slots * MAXLEN) + lax.iota(
        jnp.int32, half_slots * MAXLEN
    )
    placed = place_rows(key_value, own_slots, slot_begin, slot_size)
    return placed.reshape(1, half_slots, MAXLEN, 2, head_width)


def solution(mesh):
    return jax.shard_map(
        per_device,
        mesh=mesh,
        in_specs=(
            P(("groups", "mp", "layer", "pool"), None),
            P("layer", "pool", None, "mp"),
            P("groups"),
            P("groups"),
            P("groups"),
        ),
        out_specs=P("layer", ("groups", "pool"), None, None, "mp"),
        check_vma=False,
    )
```

```python
import functools

import jax
import jax.numpy as jnp
from jax import lax
from jax.experimental import pallas as pl
from jax.experimental.pallas import tpu as pltpu
from jax.sharding import PartitionSpec as P
MAXLEN = 128
BLANK = 16


def pack_tables(lengths, slot_of, order):
    count_all = lengths.shape[0]
    request_ids = lax.iota(jnp.int32, count_all)
    selector = (order[:, None] == request_ids[None, :]).astype(jnp.int32)
    order_length = jnp.sum(selector * lengths[None, :], axis=1)
    order_begin = jnp.cumsum(order_length) - order_length
    begins = jnp.sum(selector * order_begin[:, None], axis=0)
    owner = (slot_of[:, None] == request_ids[None, :]).astype(jnp.int32)
    request = jnp.sum(owner * request_ids[:, None], axis=0)
    chooser = (request[:, None] == request_ids[None, :]).astype(jnp.int32)
    slot_begin = jnp.sum(chooser * begins[None, :], axis=1)
    slot_size = jnp.sum(chooser * lengths[None, :], axis=1)
    return (slot_begin, slot_size)


def place_rows(values, positions, slot_begin, slot_size):
    slot_count = slot_begin.shape[0]
    slot_index = positions // MAXLEN
    offset = positions % MAXLEN
    selector = (slot_index[:, None] == lax.iota(jnp.int32, slot_count)[None, :]).astype(jnp.int32)
    first_row = jnp.sum(selector * slot_begin[None, :], axis=1)
    row_limit = jnp.sum(selector * slot_size[None, :], axis=1)
    inside = offset < row_limit
    source = jnp.where(inside, first_row + offset, 0)
    taken = jnp.take(values, source, axis=0)
    return jnp.where(inside[:, None], taken, jnp.zeros((), values.dtype))


def gather_multiply(mp_size, x_ref, w_hbm, kv_hbm, w_raw, w_flat, x_send, rows, acc, part, other, done, *sems):
    w_sem, x_ss, x_rs, r_ss, r_rs, l_ss, l_rs, p_ss, p_rs, o_sem = sems
    mesh_id = pl.DeviceIdType.MESH
    ring = 2 * mp_size
    count, half = x_send.shape
    width = w_flat.shape[1]
    pool = lax.axis_index("pool")
    layer = lax.axis_index("layer")
    mp = lax.axis_index("mp")
    here = mp + layer * (ring - 1 - 2 * mp)

    def place(steps):
        at = (here + steps + ring) % ring
        on_layer = at // mp_size
        return at + on_layer * (ring - 1 - 2 * at), on_layer

    def chip(steps):
        on_mp, on_layer = place(steps)
        return on_mp * 2 + on_layer

    def device(steps):
        on_mp, on_layer = place(steps)
        return {"mp": on_mp, "layer": on_layer}

    partner = {"pool": 1 - pool}
    depth = half // 4

    def weight_copy(i):
        return pltpu.make_async_copy(
            w_hbm.at[pl.ds(i * depth, depth)], w_raw.at[pl.ds(i * depth, depth)], w_sem.at[i]
        )

    for i in range(4):
        weight_copy(i).start()
    barrier = pltpu.get_barrier_semaphore()
    for target in (device(1), device(-1), partner):
        pl.semaphore_signal(barrier, inc=1, device_id=target, device_id_type=mesh_id)
    mine = chip(0)
    rows[mine, pool] = x_ref[:, pl.ds(pl.multiple_of(pool * half, half), half)].astype(jnp.bfloat16)
    x_send[...] = x_ref[:, pl.ds(pl.multiple_of((1 - pool) * half, half), half)].astype(jnp.bfloat16)
    pl.semaphore_wait(barrier, 3)

    def send(k, direction):
        last = k == ring - 2
        second = (k % 2 == 1) or (last and direction < 0)
        core = 1 - pool if second else pool
        slot = rows.at[chip(-direction * (k // 2)), core]
        ss, rs = (r_ss, r_rs) if direction > 0 else (l_ss, l_rs)
        return pltpu.make_async_remote_copy(
            src_ref=slot, dst_ref=slot, send_sem=ss.at[k], recv_sem=rs.at[k],
            device_id=device(direction), device_id_type=mesh_id,
        )

    def swap_rows():
        return pltpu.make_async_remote_copy(
            src_ref=x_send, dst_ref=rows.at[mine, pool], send_sem=x_ss, recv_sem=x_rs,
            device_id=partner, device_id_type=mesh_id,
        )

    def arrived(k, direction):
        last = k == ring - 2
        second = (k % 2 == 1) or (last and direction < 0)
        core = 1 - pool if second else pool
        slot = rows.at[chip(-direction * (k // 2 + 1)), core]
        ss, rs = (r_ss, r_rs) if direction > 0 else (l_ss, l_rs)
        pltpu.make_async_remote_copy(
            src_ref=slot, dst_ref=slot, send_sem=ss.at[k], recv_sem=rs.at[k],
            device_id=device(direction), device_id_type=mesh_id,
        ).wait_recv()

    def flatten(i):
        weight_copy(i).wait()
        piece = 32

        @pl.loop(0, depth // piece)
        def _(t):
            start = pl.multiple_of(i * depth + t * piece, piece)
            w_flat[pl.ds(start, piece), :] = w_raw[pl.ds(start, piece)].reshape(piece, width)

    def swap_part(m, at, side):
        return pltpu.make_async_remote_copy(
            src_ref=part.at[at, side], dst_ref=other.at[at, side],
            send_sem=p_ss.at[m, side], recv_sem=p_rs.at[m, side],
            device_id=partner, device_id_type=mesh_id,
        )

    def store(m, at):
        rows_at = pl.ds(pl.multiple_of(at * 2 * count, 2 * count), 2 * count)
        return pltpu.make_async_copy(done.at[at], kv_hbm.at[rows_at], o_sem.at[m])

    side_width = width // 2
    columns = 1024 if side_width % 1024 == 0 else 128

    def multiply(chips, m):
        for side in range(2):

            @pl.loop(0, side_width // columns)
            def _(t):
                start = pl.multiple_of(t * columns, columns)
                span = pl.ds(start, columns)
                wide = pl.ds(pl.multiple_of(side * side_width + start, columns), columns)
                left = jnp.concatenate([rows[c].reshape(2 * count, half) for c in chips], axis=0)
                product = jnp.dot(left, w_flat[:, wide], preferred_element_type=jnp.float32)
                for i, c in enumerate(chips):
                    one = product[i * 2 * count : (i + 1) * 2 * count]
                    acc[c, side, :, span] = one
                    part[c, side, :, span] = one.astype(jnp.bfloat16)

            for i, c in enumerate(chips):
                swap_part(m + i, c, side).start()

    def finish(chips, m):
        piece = 16
        for i, c in enumerate(chips):
            for side in range(2):
                swap_part(m + i, c, side).wait_recv()

            @pl.loop(0, 2 * count // piece)
            def _(t):
                span = pl.ds(pl.multiple_of(t * piece, piece), piece)
                total = [
                    (acc[c, side, span, :] + other[c, side, span, :].astype(jnp.float32)).astype(jnp.bfloat16)
                    for side in range(2)
                ]
                done[c, span] = jnp.concatenate(total, axis=1).reshape(piece, 2, side_width)

            store(m + i, c).start()

    send(0, 1).start()
    send(0, -1).start()
    swap_rows().start()
    swap_rows().wait_recv()
    send(1, 1).start()
    send(1, -1).start()
    flatten(0)
    flatten(1)
    reach = ring // 2
    waiting = None
    for k in range(ring - 1):
        if k == ring - 2:
            finish(*waiting)
        ahead = k + 2
        arrived(k, 1)
        if ahead <= ring - 2:
            send(ahead, 1).start()
        arrived(k, -1)
        if ahead < ring - 2:
            send(ahead, -1).start()
        elif ahead == ring - 1:
            send(ring - 2, -1).start()
        if k == 0:
            flatten(2)
            flatten(3)
            multiply([mine], 0)
            waiting = ([mine], 0)
        elif k % 2 == 1:
            d = (k + 1) // 2
            chips = [chip(-d), chip(d)]
            if d == 1:
                finish(*waiting)
            multiply(chips, 2 * d - 1)
            waiting = (chips, 2 * d - 1)
        elif k < ring - 2:
            finish(*waiting)
    multiply([chip(reach)], ring - 1)
    finish([chip(reach)], ring - 1)
    swap_rows().wait_send()
    for k in range(ring - 1):
        send(k, 1).wait_send()
        send(k, -1).wait_send()
    blocks = [mine]
    for d in range(1, reach):
        blocks += [chip(-d), chip(d)]
    for m, c in enumerate(blocks + [chip(reach)]):
        for side in range(2):
            swap_part(m, c, side).wait_send()
        store(m, c).wait()


def key_values(enc_rows, weight, mp_size):
    count, features = enc_rows.shape
    half, _, head_width = weight.shape
    width, ring = 2 * head_width, 2 * mp_size
    dma = pltpu.SemaphoreType.DMA
    block = (ring, 2, 2 * count, head_width)
    return pl.pallas_call(
        functools.partial(gather_multiply, mp_size),
        out_shape=jax.ShapeDtypeStruct((ring * 2 * count, 2, head_width), jnp.bfloat16),
        in_specs=[pl.BlockSpec(memory_space=pltpu.VMEM), pl.BlockSpec(memory_space=pl.ANY)],
        out_specs=pl.BlockSpec(memory_space=pl.ANY),
        scratch_shapes=[
            pltpu.VMEM(weight.shape, jnp.bfloat16),
            pltpu.VMEM((half, width), jnp.bfloat16),
            pltpu.VMEM((count, half), jnp.bfloat16),
            pltpu.VMEM((ring, 2, count, half), jnp.bfloat16),
            pltpu.VMEM(block, jnp.float32),
            pltpu.VMEM(block, jnp.bfloat16),
            pltpu.VMEM(block, jnp.bfloat16),
            pltpu.VMEM((ring, 2 * count, 2, head_width), jnp.bfloat16),
            dma((4,)),
            dma,
            dma,
            dma((ring - 1,)),
            dma((ring - 1,)),
            dma((ring - 1,)),
            dma((ring - 1,)),
            dma((ring, 2)),
            dma((ring, 2)),
            dma((ring,)),
        ],
        compiler_params=pltpu.CompilerParams(
            collective_id=0, has_side_effects=True, vmem_limit_bytes=56 << 20
        ),
        name="gather_multiply",
    )(enc_rows, weight)


def place_kernel(lengths, slot_of, order, kv_hbm, out_hbm, windows, begins, request, in_sems, out_sems):
    slot_count = lengths.shape[0]
    half_slots = windows.shape[0]
    first = lax.axis_index("pool") * half_slots

    def one(i, begin):
        begins[order[i]] = begin
        request[slot_of[i]] = i
        return begin + lengths[order[i]]

    lax.fori_loop(0, slot_count, one, jnp.int32(0))

    def lookup(s):
        who = request[first + s]
        base = jnp.minimum(begins[who], kv_hbm.shape[0] - MAXLEN)
        return lengths[who], base, begins[who] - base

    def fetch(s):
        base = lookup(s)[1]
        return pltpu.make_async_copy(
            kv_hbm.at[pl.ds(base, MAXLEN)], windows.at[s, pl.ds(0, MAXLEN)], in_sems.at[s]
        )

    def write(s):
        skip = lookup(s)[2]
        return pltpu.make_async_copy(
            windows.at[s, pl.ds(skip, MAXLEN)], out_hbm.at[0, s], out_sems.at[s]
        )

    for s in range(half_slots):
        fetch(s).start()
    blank = jnp.zeros((BLANK, *windows.shape[2:]), windows.dtype)
    for s in range(half_slots):
        size, _, skip = lookup(s)
        fetch(s).wait()

        @pl.loop(0, (MAXLEN - size + BLANK - 1) // BLANK)
        def _(j):
            windows[s, pl.ds(skip + size + j * BLANK, BLANK)] = blank

        write(s).start()
    for s in range(half_slots):
        write(s).wait()


def place_slots(key_value, lengths, slot_of, order, half_slots):
    head_width = key_value.shape[2]
    slot_count = lengths.shape[0]
    smem = pl.BlockSpec(memory_space=pltpu.SMEM)
    shape = (1, half_slots, MAXLEN, 2, head_width)
    return pl.pallas_call(
        place_kernel,
        out_shape=jax.ShapeDtypeStruct(shape, jnp.bfloat16),
        in_specs=[smem, smem, smem, pl.BlockSpec(memory_space=pl.ANY)],
        out_specs=pl.BlockSpec(memory_space=pl.ANY),
        scratch_shapes=[
            pltpu.VMEM((half_slots, 2 * MAXLEN + BLANK, 2, head_width), jnp.bfloat16),
            pltpu.SMEM((slot_count,), jnp.int32),
            pltpu.SMEM((slot_count,), jnp.int32),
            pltpu.SemaphoreType.DMA((half_slots,)),
            pltpu.SemaphoreType.DMA((half_slots,)),
        ],
        compiler_params=pltpu.CompilerParams(vmem_limit_bytes=56 << 20),
        name="place_slots",
    )(lengths, slot_of, order, key_value)


def per_device(enc_rows, kv_weight, lengths, slot_of, order):
    half_slots = lengths.shape[0] // lax.axis_size("pool")
    head_width = kv_weight.shape[3]
    mp_size = lax.axis_size("mp")
    ring_fits = (
        lax.axis_size("layer") == 2
        and lax.axis_size("pool") == 2
        and 2 <= mp_size <= 8
        and enc_rows.shape[0] % 16 == 0
        and head_width % 128 == 0
    )
    if ring_fits:
        key_value = key_values(enc_rows, kv_weight[0], mp_size)
        return place_slots(key_value, lengths, slot_of, order, half_slots)
    slot_begin, slot_size = pack_tables(lengths, slot_of, order)
    row_block = enc_rows.astype(jnp.bfloat16)
    weight = lax.all_gather(kv_weight[0], "pool", axis=0, tiled=True)
    flat_weight = weight.reshape(weight.shape[0], 2 * head_width)
    key_value = jnp.dot(
        lax.all_gather(row_block, ("mp", "layer", "pool"), axis=0, tiled=True),
        flat_weight,
        preferred_element_type=jnp.float32,
    ).astype(jnp.bfloat16)
    own_slots = lax.axis_index("pool") * (half_slots * MAXLEN) + lax.iota(
        jnp.int32, half_slots * MAXLEN
    )
    placed = place_rows(key_value, own_slots, slot_begin, slot_size)
    return placed.reshape(1, half_slots, MAXLEN, 2, head_width)


def solution(mesh):
    return jax.shard_map(
        per_device,
        mesh=mesh,
        in_specs=(
            P(("groups", "mp", "layer", "pool"), None),
            P("layer", "pool", None, "mp"),
            P("groups"),
            P("groups"),
            P("groups"),
        ),
        out_specs=P("layer", ("groups", "pool"), None, None, "mp"),
        check_vma=False,
    )
```
